32 devices in a mesh: group: 4 (over y, x), ctx: 8 (over z, core).
Axes of the slice: x: 2, y: 2, z: 4, core: 2. Of those that a mesh axis runs over, the one named last changes fastest.
Arguments:
- query: bfloat16 [128, 128, 576], P('group', 'ctx'), may hold values from -160 to 160
- cache: bfloat16 [32, 8192, 576], P('group', 'ctx'), may hold values from -6 to 6
- new_keys: bfloat16 [128, 576], P('group'), may hold values from -7 to 7
- lengths: int32 [32], P('group'), may hold values from 1 to 8192, as said below
- value_up_weight: bfloat16 [128, 512, 128], P('ctx'), may hold values from -1 to 1
- w_out: bfloat16 [16384, 7168], P('ctx'), may hold values from -0.1875 to 0.1875
- residual: bfloat16 [128, 7168], P(('group', 'ctx')), may hold values from -6 to 6
- norm_gain: float32 [7168], replicated, may hold values from 0.1 to 1.9
- w_router: bfloat16 [7168, 16], replicated, may hold values from -0.125 to 0.125
- routes: int32 [128, 8], P(('group', 'ctx')), may hold values from 0 to 15, all different within a row
- w_gate: bfloat16 [7168, 32768], P(None, ('group', 'ctx')), may hold values from -0.0625 to 0.0625
- w_up: bfloat16 [7168, 32768], P(None, ('group', 'ctx')), may hold values from -0.0625 to 0.0625
- w_down: bfloat16 [32768, 7168], P(('group', 'ctx')), may hold values from -0.125 to 0.125
Outputs:
- attn_out: bfloat16 [128, 7168], P(('group', 'ctx'))
- layer_out: bfloat16 [128, 7168], P(('group', 'ctx'))
The draws below stay inside these ranges and needn't reach their ends.
Inputs may be any that keep to these rules, and one draw needn't show every extreme that they name: `lengths`: some request has all 8192 positions live.
All inputs are finite; a program needn't handle non-finite values.
Results may differ from the reference program's by a relative error of at most 0.018.
Values may be sent and summed in bfloat16 or wider, within the bound.
A program may use at most 192 MiB of HBM per device.

```python
import jax
import jax.numpy as jnp
from jax import lax

D = 7168
HEAD_COUNT = 128
LATENT_WIDTH = 512
ROTARY_WIDTH = 64
QK_NOPE = 128
VALUE_HEAD_WIDTH = 128
FF_E = 2048
TOPK = 8
EXPERTS = 16
QPR = 4
S_DEV = 1024
LAT = 576
REQS = 32
QUERY_ROW_TOTAL = 128
LEN = 8192
N_CTX = 8


def draw_query(key, part):
    noise_key = jax.random.fold_in(key, 1)
    value_rows = jnp.clip(jax.random.normal(noise_key, (QUERY_ROW_TOTAL, HEAD_COUNT, LAT), jnp.float32), -5.0, 5.0) * 0.8
    return value_rows.astype(jnp.bfloat16)


def draw_cache(key, part):
    noise_key = jax.random.fold_in(key, 2)
    value_rows = jnp.clip(jax.random.normal(noise_key, (REQS, LEN, LAT), jnp.float32), -5.0, 5.0)
    return value_rows.astype(jnp.bfloat16)


def draw_new_keys(key, part):
    noise_key = jax.random.fold_in(key, 3)
    value_rows = jnp.clip(jax.random.normal(noise_key, (QUERY_ROW_TOTAL, LAT), jnp.float32), -5.0, 5.0)
    return value_rows.astype(jnp.bfloat16)


def draw_lengths(key, part):
    length_key, second = jax.random.split(jax.random.fold_in(key, 4))
    value_rows = jax.random.randint(length_key, (REQS,), 1, LEN + 1, dtype=jnp.int32)
    long_spot = jax.random.randint(second, (), 0, REQS, dtype=jnp.int32)
    return jnp.where(jnp.arange(REQS, dtype=jnp.int32) == long_spot, LEN, value_rows).astype(jnp.int32)


def steps_of(key, dims, shards, least, top_value):
    def one(position, parts):
        draws = jax.random.uniform(jax.random.fold_in(jax.random.fold_in(key, 6), position), (parts,), jnp.float32, least / len(shards), top_value / len(shards))
        return jnp.repeat(jnp.exp(draws), dims[position] // parts).reshape((-1,) + (1,) * (len(dims) - position - 1))

    gain = one(*shards[0])
    for cut in shards[1:]:
        gain = gain * one(*cut)
    return gain


def picks_of(rng, rows, number_of, top, lift):
    sequence = jax.random.permutation(jax.random.fold_in(rng, 1), number_of)
    favour = sequence
    for power in range(3):
        favour = favour * favour // number_of
    favour = favour * lift // number_of
    tickets = jax.random.randint(jax.random.fold_in(rng, 2), (rows, number_of), 0, 4096) + favour
    fixed_rows = jax.random.permutation(jax.random.fold_in(rng, 3), rows)[jnp.arange(number_of) % rows]
    tickets = jnp.where(jnp.arange(rows)[:, None] == fixed_rows[None, :], 1 << 14, tickets)
    merit = tickets * number_of + jnp.arange(number_of)
    return lax.top_k(merit.astype(jnp.int32), top)[1].astype(jnp.int32)


def scatter_about(rng, shape, spread, reach, cuts=(), held_as=jnp.bfloat16):
    array = jax.random.normal(rng, shape, jnp.float32) * spread
    if len(cuts) > 0:
        array = steps_of(rng, shape, cuts, -0.22, 0.18) * array
    return jnp.clip(array, min=-reach, max=reach).astype(held_as)


def setup_inputs(seed: int = 0) -> dict:
    key_of = jax.random.split(jax.random.key(seed), 14)
    query = draw_query(jax.random.fold_in(key_of[13], 71), 0)
    cache = draw_cache(jax.random.fold_in(key_of[13], 71), 0)
    new_keys = draw_new_keys(jax.random.fold_in(key_of[13], 71), 0)
    lengths = draw_lengths(jax.random.fold_in(key_of[13], 71), 0)
    value_up_weight = scatter_about(key_of[4], (HEAD_COUNT, LATENT_WIDTH, VALUE_HEAD_WIDTH), (LATENT_WIDTH // 16) ** -0.5, 1.0, ((0, 8),))
    w_out = scatter_about(key_of[5], (HEAD_COUNT * VALUE_HEAD_WIDTH, D), (HEAD_COUNT * VALUE_HEAD_WIDTH // 16) ** -0.5, 0.1875, ((0, 8),))
    residual = scatter_about(key_of[6], (QUERY_ROW_TOTAL, D), 1.0, 6.0, ((0, 32),))
    norm_gain = jnp.clip(1.0 + 0.18 * jax.random.normal(key_of[7], (D,), jnp.float32), 0.1, 1.9)
    w_router = scatter_about(key_of[8], (D, EXPERTS), (D // 4) ** -0.5, 0.125)
    routes = picks_of(key_of[9], QUERY_ROW_TOTAL, EXPERTS, TOPK, 4096)
    w_gate = scatter_about(key_of[10], (D, EXPERTS * FF_E), D ** -0.5, 0.0625, ((1, 32),))
    w_up = scatter_about(key_of[11], (D, EXPERTS * FF_E), D ** -0.5, 0.0625, ((1, 32),))
    w_down = scatter_about(key_of[12], (EXPERTS * FF_E, D), FF_E ** -0.5, 0.125, ((0, 32),))
    return {"query": query, "cache": cache, "new_keys": new_keys, "lengths": lengths, "value_up_weight": value_up_weight, "w_out": w_out, "residual": residual, "norm_gain": norm_gain, "w_router": w_router, "routes": routes, "w_gate": w_gate, "w_up": w_up, "w_down": w_down}


neg_floor = -1e+30
route_scale = 2.5
norm_eps = 1e-06

def request_latent(query_rows, cache_rows, recent_keys, length):
    score_scale = (QK_NOPE + ROTARY_WIDTH) ** (-0.5)
    query_wide = query_rows.astype(jnp.float32)
    block_list = cache_rows.reshape(N_CTX, S_DEV, LAT).astype(jnp.float32)
    positions = jnp.arange(LEN, dtype=jnp.int32).reshape(N_CTX, S_DEV)
    live_mask = (positions < length)[:, None, None, :]
    scores = score_scale * jnp.einsum('qhd,btd->bqht', query_wide, block_list, precision=lax.Precision.HIGHEST)
    block_max = lax.optimization_barrier(jnp.max(jnp.where(live_mask, scores, neg_floor), axis=-1))
    probability = jnp.exp(jnp.where(live_mask, scores - block_max[..., None], neg_floor))
    block_sum = lax.optimization_barrier(jnp.sum(probability, axis=-1))
    rounded_width = lax.optimization_barrier(probability.astype(jnp.bfloat16)).astype(jnp.float32)
    block_result = jnp.einsum('arij,ajx->arix', rounded_width, block_list[:, :, :LATENT_WIDTH], precision=lax.Precision.HIGHEST)
    recent_wide_keys = recent_keys.astype(jnp.float32)
    near_scores = score_scale * jnp.einsum('qhd,jd->qhj', query_wide, recent_wide_keys, precision=lax.Precision.HIGHEST)
    causal = (jnp.arange(QPR, dtype=jnp.int32)[None, :] <= jnp.arange(QPR, dtype=jnp.int32)[:, None])[:, None, :]
    near_max = lax.optimization_barrier(jnp.max(jnp.where(causal, near_scores, neg_floor), axis=-1))
    joint_max = jnp.maximum(lax.optimization_barrier(jnp.max(block_max, axis=0)), near_max)
    block_rescale = jnp.exp(block_max - joint_max[None])
    nearby_probability = jnp.exp(jnp.where(causal, near_scores - joint_max[..., None], neg_floor))
    denominator = lax.optimization_barrier(jnp.sum(block_rescale * block_sum, axis=0)) + lax.optimization_barrier(jnp.sum(nearby_probability, axis=-1))
    softmax_numerator = lax.optimization_barrier(jnp.sum(block_rescale[..., None] * block_result, axis=0)) + jnp.einsum('pbl,lv->pbv', nearby_probability, recent_wide_keys[:, :LATENT_WIDTH], precision=lax.Precision.HIGHEST)
    return (softmax_numerator / denominator[..., None]).astype(jnp.bfloat16)

def reference(query, cache, new_keys, lengths, value_up_weight, w_out, residual, norm_gain, w_router, routes, w_gate, w_up, w_down):
    query_grid = query.reshape(REQS, QPR, HEAD_COUNT, LAT)
    fresh_grid = new_keys.reshape(REQS, QPR, LAT)
    latent_vector = lax.map(lambda packed: request_latent(packed[0], packed[1], packed[2], packed[3]), (query_grid, cache, fresh_grid, lengths))
    latent_vector = latent_vector.reshape(QUERY_ROW_TOTAL, HEAD_COUNT, LATENT_WIDTH)
    per_head_values = jnp.einsum('gxj,xjs->gxs', latent_vector.astype(jnp.float32), value_up_weight.astype(jnp.float32), precision=lax.Precision.HIGHEST).astype(jnp.bfloat16)
    attention = jnp.dot(per_head_values.reshape(QUERY_ROW_TOTAL, HEAD_COUNT * VALUE_HEAD_WIDTH), w_out, preferred_element_type=jnp.float32)
    attn_out = attention.astype(jnp.bfloat16)
    stream = (residual.astype(jnp.float32) + attention).astype(jnp.bfloat16)
    stream_wide = stream.astype(jnp.float32)
    mean_square = lax.optimization_barrier(jnp.mean(stream_wide * stream_wide, axis=-1, keepdims=True))
    normed = (stream_wide * lax.rsqrt(mean_square + norm_eps) * norm_gain).astype(jnp.bfloat16)
    gate_values = jax.nn.sigmoid(jnp.dot(normed, w_router, preferred_element_type=jnp.float32))
    selected_experts = (routes[:, :, None] == jnp.arange(EXPERTS, dtype=jnp.int32)[None, None, :]).astype(jnp.float32)
    picked = lax.optimization_barrier(jnp.sum(selected_experts * gate_values[:, None, :], axis=-1))
    route_weights = route_scale * picked / lax.optimization_barrier(jnp.sum(picked, axis=-1, keepdims=True))
    coefficient = lax.optimization_barrier(jnp.sum(route_weights[:, :, None] * selected_experts, axis=1))
    expert_mix = jnp.zeros((QUERY_ROW_TOTAL, D), jnp.float32)
    for expert in range(EXPERTS):
        columns = slice(expert * FF_E, (expert + 1) * FF_E)
        gate_sum = jnp.dot(normed, w_gate[:, columns], preferred_element_type=jnp.float32)
        up_sum = jnp.dot(normed, w_up[:, columns], preferred_element_type=jnp.float32)
        hidden = (jax.nn.silu(gate_sum) * up_sum).astype(jnp.bfloat16)
        expert_out = jnp.dot(hidden, w_down[columns, :], preferred_element_type=jnp.float32)
        expert_mix = expert_mix + coefficient[:, expert:expert + 1] * expert_out
    layer_out = (stream_wide + expert_mix).astype(jnp.bfloat16)
    return (attn_out, layer_out)
```

```python
import functools

import jax
import jax.numpy as jnp
from jax import lax
from jax.experimental import pallas as pl
from jax.experimental.pallas import tpu as pltpu
from jax.sharding import PartitionSpec as P

LATENT_WIDTH = 512
ROTARY_WIDTH = 64
QK_NOPE = 128
VALUE_HEAD_WIDTH = 128
EXPERTS = 16
LANES = 128
MESH = pl.DeviceIdType.MESH


neg_floor = -1e30
route_scale = 2.5
norm_eps = 1e-06


def enter(peers):
    barrier = pltpu.get_barrier_semaphore()
    for peer in peers:
        pl.semaphore_signal(barrier, inc=1, device_id=peer, device_id_type=MESH)
    pl.semaphore_wait(barrier, len(peers))


def place(planes, depth):
    g = lax.axis_index("group")
    c = lax.axis_index("ctx")
    z, k = c // 2, c % 2
    partner = (g, z * 2 + 1 - k)
    plane = [(lax.rem(g + d, lax.axis_size("group")), c) for d in range(1, planes)]
    line = [(g, lax.rem(z + d, depth) * 2 + k) for d in range(1, depth)]
    return g, z, k, partner, plane, line


def gather_kernel(planes, depth, x_ref, out_ref, core_send, core_recv, plane_send, plane_recv, line_send, line_recv):
    g, z, k, partner, plane, line = place(planes, depth)
    enter([partner] + plane + line)
    out_ref[k, g, z] = x_ref[...]

    def line_copy(d, slot):
        return pltpu.make_async_remote_copy(
            src_ref=x_ref, dst_ref=slot, send_sem=line_send.at[d], recv_sem=line_recv.at[d],
            device_id=line[d - 1], device_id_type=MESH)

    def plane_copy(p, d, src, slot):
        return pltpu.make_async_remote_copy(
            src_ref=src, dst_ref=slot, send_sem=plane_send.at[p, d], recv_sem=plane_recv.at[p, d],
            device_id=plane[p - 1], device_id_type=MESH)

    def core_copy(p, d, src, slot):
        return pltpu.make_async_remote_copy(
            src_ref=src, dst_ref=slot, send_sem=core_send.at[p, d], recv_sem=core_recv.at[p, d],
            device_id=partner, device_id_type=MESH)

    sent = []
    for d in range(1, depth):
        copy = line_copy(d, out_ref.at[k, g, z])
        copy.start()
        sent.append(copy)
    for d in range(depth):
        zd = lax.rem(z - d + depth, depth)
        slot = out_ref.at[k, g, zd]
        src = x_ref if d == 0 else slot
        if d > 0:
            line_copy(d, slot).wait_recv()
        for p in range(1, planes):
            copy = plane_copy(p, d, src, slot)
            copy.start()
            sent.append(copy)
        copy = core_copy(0, d, src, slot)
        copy.start()
        sent.append(copy)
    for d in range(depth):
        zd = lax.rem(z - d + depth, depth)
        for p in range(1, planes):
            slot = out_ref.at[k, lax.rem(g - p + planes, planes), zd]
            plane_copy(p, d, slot, slot).wait_recv()
            copy = core_copy(p, d, slot, slot)
            copy.start()
            sent.append(copy)
    for d in range(depth):
        zd = lax.rem(z - d + depth, depth)
        for p in range(planes):
            slot = out_ref.at[1 - k, lax.rem(g - p + planes, planes), zd]
            core_copy(p, d, slot, slot).wait_recv()
    for copy in sent:
        copy.wait_send()


def all_rows(x, planes, depth, collective_id):
    sems = pltpu.SemaphoreType.DMA
    return pl.pallas_call(
        functools.partial(gather_kernel, planes, depth),
        out_shape=jax.ShapeDtypeStruct((2, planes, depth) + x.shape, x.dtype),
        in_specs=[pl.BlockSpec(memory_space=pltpu.VMEM)],
        out_specs=pl.BlockSpec(memory_space=pltpu.VMEM),
        scratch_shapes=[sems((planes, depth))] * 4 + [sems((depth,))] * 2,
        compiler_params=pltpu.CompilerParams(
            collective_id=collective_id, has_side_effects=True, vmem_limit_bytes=32 * 2**20),
    )(x)


def scatter_kernel(planes, depth, x_ref, out_ref, core_buf, plane_out, plane_buf, line_out, line_buf,
                   core_send, core_recv, plane_send, plane_recv, line_send, line_recv):
    g, z, k, partner, plane, line = place(planes, depth)
    enter([partner] + plane + line)
    at = g if planes > 1 else 0
    wide = lambda block: block.astype(jnp.float32)

    sent = []
    order = list(range(1, planes)) + [0]
    core = {}
    for p in order:
        gp = lax.rem(at + p, planes)
        copy = pltpu.make_async_remote_copy(
            src_ref=x_ref.at[1 - k, gp], dst_ref=core_buf.at[p], send_sem=core_send.at[p], recv_sem=core_recv.at[p],
            device_id=partner, device_id_type=MESH)
        copy.start()
        core[p] = copy
        sent.append(copy)
    planes_in = {}
    for p in order[:-1]:
        gp = lax.rem(at + p, planes)
        core[p].wait_recv()
        for d in range(depth):
            plane_out[p, d] = (wide(x_ref[k, gp, d]) + wide(core_buf[p, d])).astype(plane_out.dtype)
        copy = pltpu.make_async_remote_copy(
            src_ref=plane_out.at[p], dst_ref=plane_buf.at[p], send_sem=plane_send.at[p], recv_sem=plane_recv.at[p],
            device_id=plane[p - 1], device_id_type=MESH)
        copy.start()
        planes_in[p] = copy
        sent.append(copy)
    core[0].wait_recv()
    for p in order[:-1]:
        planes_in[p].wait_recv()

    def total(zd):
        block = wide(x_ref[k, at, zd]) + wide(core_buf[0, zd])
        for p in range(1, planes):
            block = block + wide(plane_buf[p, zd])
        return block

    lines_in = []
    for d in range(1, depth):
        line_out[d] = total(lax.rem(z + d, depth)).astype(line_out.dtype)
        copy = pltpu.make_async_remote_copy(
            src_ref=line_out.at[d], dst_ref=line_buf.at[d], send_sem=line_send.at[d], recv_sem=line_recv.at[d],
            device_id=line[d - 1], device_id_type=MESH)
        copy.start()
        lines_in.append(copy)
        sent.append(copy)
    result = total(z)
    for d in range(1, depth):
        lines_in[d - 1].wait_recv()
        result = result + wide(line_buf[d])
    out_ref[...] = result
    for copy in sent:
        copy.wait_send()


def summed_rows(x, collective_id):
    _, planes, depth, *block = x.shape
    block = tuple(block)
    sems = pltpu.SemaphoreType.DMA
    return pl.pallas_call(
        functools.partial(scatter_kernel, planes, depth),
        out_shape=jax.ShapeDtypeStruct(block, jnp.float32),
        in_specs=[pl.BlockSpec(memory_space=pltpu.VMEM)],
        out_specs=pl.BlockSpec(memory_space=pltpu.VMEM),
        scratch_shapes=[
            pltpu.VMEM((planes, depth) + block, x.dtype),
            pltpu.VMEM((planes, depth) + block, x.dtype),
            pltpu.VMEM((planes, depth) + block, x.dtype),
            pltpu.VMEM((depth,) + block, x.dtype),
            pltpu.VMEM((depth,) + block, x.dtype),
        ] + [sems((planes,))] * 4 + [sems((depth,))] * 2,
        compiler_params=pltpu.CompilerParams(
            collective_id=collective_id, has_side_effects=True, vmem_limit_bytes=32 * 2**20),
    )(x)


def local(
    query,
    cache,
    new_keys,
    lengths,
    value_up_weight,
    w_out,
    residual,
    norm_gain,
    w_router,
    routes,
    w_gate,
    w_up,
    w_down,
):
    score_scale = (QK_NOPE + ROTARY_WIDTH) ** (-0.5)
    ctx_count = lax.axis_size("ctx")
    group_count = lax.axis_size("group")
    depth = ctx_count // 2
    ctx_index = lax.axis_index("ctx")
    group_index = lax.axis_index("group")
    grouped_rows, local_heads, features = query.shape
    request_batch = lengths.shape[0]
    draft_tokens = grouped_rows // request_batch
    block_len = cache.shape[1]
    all_routes = lax.all_gather(routes, ("group", "ctx"), axis=0, tiled=True)
    positions = ctx_index * block_len + jnp.arange(block_len, dtype=jnp.int32)
    live_mask = (positions[None, :] < lengths[:, None])[:, None, None, :]
    compressed_keys = cache[:, :, :LATENT_WIDTH]
    all_heads = lax.all_gather(query, "ctx", axis=1, tiled=True)
    current_width = all_heads.shape[1]
    shaped = all_heads.reshape(request_batch, draft_tokens, current_width, features)
    scores = score_scale * jnp.einsum(
        "rqhd,rtd->rqht", shaped, cache, preferred_element_type=jnp.float32
    )
    block_max = jnp.max(jnp.where(live_mask, scores, neg_floor), axis=-1)
    probability = jnp.exp(jnp.where(live_mask, scores - block_max[..., None], neg_floor))
    block_sum = jnp.sum(probability, axis=-1)
    block_result = jnp.einsum(
        "rqht,rtk->rqhk",
        probability.astype(jnp.bfloat16),
        compressed_keys,
        preferred_element_type=jnp.float32,
    ).astype(jnp.bfloat16)
    swap = functools.partial(lax.all_to_all, axis_name="ctx", split_axis=2, concat_axis=0, tiled=True)
    arrived = (
        swap(block_max.reshape(grouped_rows, current_width)[None]),
        swap(block_sum.reshape(grouped_rows, current_width)[None]),
        swap(block_result.reshape(grouped_rows, current_width, LATENT_WIDTH)[None]),
    )
    cache_max = jnp.max(arrived[0], axis=0)
    factors = jnp.exp(arrived[0] - cache_max[None])
    cache_sum = jnp.sum(factors * arrived[1], axis=0)
    cache_result = jnp.sum(factors[..., None] * arrived[2].astype(jnp.float32), axis=0)
    own_query = query.reshape(request_batch, draft_tokens, local_heads, features)
    recent_keys = new_keys.reshape(request_batch, draft_tokens, features)
    near_scores = score_scale * jnp.einsum(
        "rqhd,rjd->rqhj", own_query, recent_keys, preferred_element_type=jnp.float32
    )
    causal = (
        jnp.arange(draft_tokens, dtype=jnp.int32)[None, :]
        <= jnp.arange(draft_tokens, dtype=jnp.int32)[:, None]
    )
    causal = causal[None, :, None, :]
    near_max = jnp.max(jnp.where(causal, near_scores, neg_floor), axis=-1)
    shaped_max = cache_max.reshape(request_batch, draft_tokens, local_heads)
    joint_max = jnp.maximum(shaped_max, near_max)
    cache_rescale = jnp.exp(shaped_max - joint_max)
    nearby_probability = jnp.exp(jnp.where(causal, near_scores - joint_max[..., None], neg_floor))
    denominator = cache_sum.reshape(
        request_batch, draft_tokens, local_heads
    ) * cache_rescale + jnp.sum(nearby_probability, axis=-1)
    softmax_numerator = cache_result.reshape(
        request_batch, draft_tokens, local_heads, LATENT_WIDTH
    ) * cache_rescale[..., None] + jnp.einsum(
        "rqhj,rjk->rqhk",
        nearby_probability,
        recent_keys[:, :, :LATENT_WIDTH].astype(jnp.float32),
        precision=lax.Precision.HIGHEST,
    )
    latent_vector = (
        (softmax_numerator / denominator[..., None])
        .astype(jnp.bfloat16)
        .reshape(grouped_rows, local_heads, LATENT_WIDTH)
    )
    per_head_values = jnp.einsum(
        "gxj,xjs->gxs", latent_vector, value_up_weight, preferred_element_type=jnp.float32
    )
    per_head_values = per_head_values.astype(jnp.bfloat16).reshape(
        grouped_rows, local_heads * VALUE_HEAD_WIDTH
    )
    row_count, model_width = residual.shape
    block = row_count * model_width // LANES
    share = jnp.dot(per_head_values, w_out, preferred_element_type=jnp.float32).astype(jnp.bfloat16)
    share = share.reshape(1, depth, 2, block, LANES).transpose(2, 0, 1, 3, 4)
    attention = summed_rows(share, 0).reshape(row_count, model_width)
    attn_out = attention.astype(jnp.bfloat16)
    stream = (residual.astype(jnp.float32) + attention).astype(jnp.bfloat16)
    stream_wide = stream.astype(jnp.float32)
    mean_square = jnp.mean(stream_wide * stream_wide, axis=-1, keepdims=True)
    normed = (stream_wide * lax.rsqrt(mean_square + norm_eps) * norm_gain).astype(jnp.bfloat16)
    rows = all_rows(normed.reshape(block, LANES), group_count, depth, 1)
    device_count = group_count * ctx_count
    rows = rows.transpose(1, 2, 0, 3, 4).reshape(device_count * row_count, model_width)
    gate_values = jax.nn.sigmoid(jnp.dot(rows, w_router, preferred_element_type=jnp.float32))
    expert_ids = jnp.arange(EXPERTS, dtype=jnp.int32)
    chosen = jnp.sum((all_routes[:, :, None] == expert_ids).astype(jnp.float32), axis=1)
    picked = chosen * gate_values
    expert = (group_index * ctx_count + ctx_index) // (device_count // EXPERTS)
    own = (expert_ids == expert).astype(jnp.float32)
    coefficient = (
        route_scale * jnp.sum(picked * own, axis=-1, keepdims=True) / jnp.sum(picked, axis=-1, keepdims=True)
    )
    gate_sum = jnp.dot(rows, w_gate, preferred_element_type=jnp.float32)
    up_sum = jnp.dot(rows, w_up, preferred_element_type=jnp.float32)
    hidden = (jax.nn.silu(gate_sum) * up_sum).astype(jnp.bfloat16)
    mixed = coefficient * jnp.dot(hidden, w_down, preferred_element_type=jnp.float32)
    mixed = mixed.astype(jnp.bfloat16).reshape(group_count, depth, 2, block, LANES)
    expert_mix = summed_rows(mixed.transpose(2, 0, 1, 3, 4), 2).reshape(row_count, model_width)
    layer_out = (stream_wide + expert_mix).astype(jnp.bfloat16)
    return (attn_out, layer_out)


def solution(mesh):
    return jax.shard_map(
        local,
        mesh=mesh,
        in_specs=(
            P("group", "ctx", None),
            P("group", "ctx", None),
            P("group", None),
            P("group"),
            P("ctx", None, None),
            P("ctx", None),
            P(("group", "ctx"), None),
            P(),
            P(),
            P(("group", "ctx"), None),
            P(None, ("group", "ctx")),
            P(None, ("group", "ctx")),
            P(("group", "ctx"), None),
        ),
        out_specs=(P(("group", "ctx"), None), P(("group", "ctx"), None)),
        check_vma=False,
    )
```

```python
import functools

import jax
import jax.numpy as jnp
from jax import lax
from jax.experimental import pallas as pl
from jax.experimental.pallas import tpu as pltpu
from jax.sharding import PartitionSpec as P

LATENT_WIDTH = 512
ROTARY_WIDTH = 64
QK_NOPE = 128
VALUE_HEAD_WIDTH = 128
EXPERTS = 16
LANES = 128
MESH = pl.DeviceIdType.MESH


neg_floor = -1e30
route_scale = 2.5
norm_eps = 1e-06


def enter(peers):
    barrier = pltpu.get_barrier_semaphore()
    for peer in peers:
        pl.semaphore_signal(barrier, inc=1, device_id=peer, device_id_type=MESH)
    pl.semaphore_wait(barrier, len(peers))


def place(planes, depth):
    g = lax.axis_index("group")
    c = lax.axis_index("ctx")
    z, k = c // 2, c % 2
    partner = (g, z * 2 + 1 - k)
    plane = [(lax.rem(g + d, lax.axis_size("group")), c) for d in range(1, planes)]
    line = [(g, lax.rem(z + d, depth) * 2 + k) for d in range(1, depth)]
    return g, z, k, partner, plane, line


def gather_kernel(planes, depth, x_ref, out_ref, core_send, core_recv, plane_send, plane_recv, line_send, line_recv):
    g, z, k, partner, plane, line = place(planes, depth)
    enter([partner] + plane + line)
    out_ref[k, g, z] = x_ref[...]

    def line_copy(d, slot):
        return pltpu.make_async_remote_copy(
            src_ref=x_ref, dst_ref=slot, send_sem=line_send.at[d], recv_sem=line_recv.at[d],
            device_id=line[d - 1], device_id_type=MESH)

    def plane_copy(p, d, src, slot):
        return pltpu.make_async_remote_copy(
            src_ref=src, dst_ref=slot, send_sem=plane_send.at[p, d], recv_sem=plane_recv.at[p, d],
            device_id=plane[p - 1], device_id_type=MESH)

    def core_copy(p, d, src, slot):
        return pltpu.make_async_remote_copy(
            src_ref=src, dst_ref=slot, send_sem=core_send.at[p, d], recv_sem=core_recv.at[p, d],
            device_id=partner, device_id_type=MESH)

    sent = []
    for d in range(1, depth):
        copy = line_copy(d, out_ref.at[k, g, z])
        copy.start()
        sent.append(copy)
    for d in range(depth):
        zd = lax.rem(z - d + depth, depth)
        slot = out_ref.at[k, g, zd]
        src = x_ref if d == 0 else slot
        if d > 0:
            line_copy(d, slot).wait_recv()
        for p in range(1, planes):
            copy = plane_copy(p, d, src, slot)
            copy.start()
            sent.append(copy)
        copy = core_copy(0, d, src, slot)
        copy.start()
        sent.append(copy)
    for d in range(depth):
        zd = lax.rem(z - d + depth, depth)
        for p in range(1, planes):
            slot = out_ref.at[k, lax.rem(g - p + planes, planes), zd]
            plane_copy(p, d, slot, slot).wait_recv()
            copy = core_copy(p, d, slot, slot)
            copy.start()
            sent.append(copy)
    for d in range(depth):
        zd = lax.rem(z - d + depth, depth)
        for p in range(planes):
            slot = out_ref.at[1 - k, lax.rem(g - p + planes, planes), zd]
            core_copy(p, d, slot, slot).wait_recv()
    for copy in sent:
        copy.wait_send()


def all_rows(x, planes, depth, collective_id):
    sems = pltpu.SemaphoreType.DMA
    return pl.pallas_call(
        functools.partial(gather_kernel, planes, depth),
        out_shape=jax.ShapeDtypeStruct((2, planes, depth) + x.shape, x.dtype),
        in_specs=[pl.BlockSpec(memory_space=pltpu.VMEM)],
        out_specs=pl.BlockSpec(memory_space=pltpu.VMEM),
        scratch_shapes=[sems((planes, depth))] * 4 + [sems((depth,))] * 2,
        compiler_params=pltpu.CompilerParams(
            collective_id=collective_id, has_side_effects=True, vmem_limit_bytes=32 * 2**20),
    )(x)


def scatter_kernel(planes, depth, x_ref, out_ref, core_buf, plane_out, plane_buf, line_out, line_buf,
                   core_send, core_recv, plane_send, plane_recv, line_send, line_recv):
    g, z, k, partner, plane, line = place(planes, depth)
    enter([partner] + plane + line)
    at = g if planes > 1 else 0
    wide = lambda block: block.astype(jnp.float32)

    sent = []
    order = list(range(1, planes)) + [0]
    core = {}
    for p in order:
        gp = lax.rem(at + p, planes)
        copy = pltpu.make_async_remote_copy(
            src_ref=x_ref.at[1 - k, gp], dst_ref=core_buf.at[p], send_sem=core_send.at[p], recv_sem=core_recv.at[p],
            device_id=partner, device_id_type=MESH)
        copy.start()
        core[p] = copy
        sent.append(copy)
    planes_in = {}
    for p in order[:-1]:
        gp = lax.rem(at + p, planes)
        core[p].wait_recv()
        for d in range(depth):
            plane_out[p, d] = (wide(x_ref[k, gp, d]) + wide(core_buf[p, d])).astype(plane_out.dtype)
        copy = pltpu.make_async_remote_copy(
            src_ref=plane_out.at[p], dst_ref=plane_buf.at[p], send_sem=plane_send.at[p], recv_sem=plane_recv.at[p],
            device_id=plane[p - 1], device_id_type=MESH)
        copy.start()
        planes_in[p] = copy
        sent.append(copy)
    core[0].wait_recv()
    for p in order[:-1]:
        planes_in[p].wait_recv()

    def total(zd):
        block = wide(x_ref[k, at, zd]) + wide(core_buf[0, zd])
        for p in range(1, planes):
            block = block + wide(plane_buf[p, zd])
        return block

    lines_in = []
    for d in range(1, depth):
        line_out[d] = total(lax.rem(z + d, depth)).astype(line_out.dtype)
        copy = pltpu.make_async_remote_copy(
            src_ref=line_out.at[d], dst_ref=line_buf.at[d], send_sem=line_send.at[d], recv_sem=line_recv.at[d],
            device_id=line[d - 1], device_id_type=MESH)
        copy.start()
        lines_in.append(copy)
        sent.append(copy)
    result = total(z)
    for d in range(1, depth):
        lines_in[d - 1].wait_recv()
        result = result + wide(line_buf[d])
    out_ref[...] = result
    for copy in sent:
        copy.wait_send()


def summed_rows(x, collective_id):
    _, planes, depth, *block = x.shape
    block = tuple(block)
    sems = pltpu.SemaphoreType.DMA
    return pl.pallas_call(
        functools.partial(scatter_kernel, planes, depth),
        out_shape=jax.ShapeDtypeStruct(block, jnp.float32),
        in_specs=[pl.BlockSpec(memory_space=pltpu.VMEM)],
        out_specs=pl.BlockSpec(memory_space=pltpu.VMEM),
        scratch_shapes=[
            pltpu.VMEM((planes, depth) + block, x.dtype),
            pltpu.VMEM((planes, depth) + block, x.dtype),
            pltpu.VMEM((planes, depth) + block, x.dtype),
            pltpu.VMEM((depth,) + block, x.dtype),
            pltpu.VMEM((depth,) + block, x.dtype),
        ] + [sems((planes,))] * 4 + [sems((depth,))] * 2,
        compiler_params=pltpu.CompilerParams(
            collective_id=collective_id, has_side_effects=True, vmem_limit_bytes=32 * 2**20),
    )(x)


def attend_kernel(depth, scale, q_ref, cache_ref, live_ref, got_ref, got_stat_ref, heads, part, stat, core_part, core_stat,
                  merged, merged_stat, q_line_send, q_line_recv, q_core_send, q_core_recv, core_send, core_recv,
                  line_send, line_recv):
    g = lax.axis_index("group")
    c = lax.axis_index("ctx")
    z, k = c // 2, c % 2
    requests, rows, _ = q_ref.shape
    spread = lax.broadcasted_iota(jnp.int32, (rows, LANES), 1)

    def chip(t):
        at, bit = z, 1
        while bit <= t:
            if t & bit:
                at = at + bit - 2 * bit * ((z // bit) % 2)
            bit *= 2
        return at

    partner = (g, z * 2 + 1 - k)
    owners = [(g, chip(t) * 2 + k) for t in range(depth)]
    enter([partner] + owners[1:])

    def remote(src, dst, send, recv, device):
        return pltpu.make_async_remote_copy(
            src_ref=src, dst_ref=dst, send_sem=send, recv_sem=recv, device_id=device, device_id_type=MESH)

    sent = []

    def go(copy):
        copy.start()
        sent.append(copy)

    def held(t):
        return q_ref if t == 0 else heads.at[t, k]

    def q_line(t):
        bit = 1 << (t.bit_length() - 1)
        return remote(held(t - bit), heads.at[t, k], q_line_send.at[t], q_line_recv.at[t], owners[bit])

    def q_core(t, half):
        return remote(held(t), heads.at[t, half], q_core_send.at[t], q_core_recv.at[t], partner)

    def results(t, half):
        return (
            remote(part.at[t, half], core_part.at[t], core_send.at[t, 0], core_recv.at[t, 0], partner),
            remote(stat.at[t, half], core_stat.at[t], core_send.at[t, 1], core_recv.at[t, 1], partner),
        )

    def returns(t):
        return (
            remote(merged.at[t], got_ref.at[t], line_send.at[t, 0], line_recv.at[t, 0], owners[t]),
            remote(merged_stat.at[t], got_stat_ref.at[t], line_send.at[t, 1], line_recv.at[t, 1], owners[t]),
        )

    def forward(t):
        go(q_core(t, k))
        bit = 1 if t == 0 else 1 << t.bit_length()
        while t + bit < depth:
            go(q_line(t + bit))
            bit *= 2

    def one(t, r):
        both = jnp.concatenate([heads[t, 0, r], heads[t, 1, r]], axis=0)
        keys = cache_ref[r]
        score = scale * lax.dot_general(both, keys, (((1,), (1,)), ((), ())), preferred_element_type=jnp.float32)
        live = live_ref[r] > 0.0
        top = jnp.max(jnp.where(live, score, neg_floor), axis=-1, keepdims=True)
        prob = jnp.exp(jnp.where(live, score - top, neg_floor))
        total = jnp.sum(prob, axis=-1, keepdims=True)
        out = jnp.dot(prob.astype(jnp.bfloat16), keys[:, :LATENT_WIDTH], preferred_element_type=jnp.float32)
        out = out.astype(part.dtype)
        for half in range(2):
            span = slice(half * rows, (half + 1) * rows)
            part[t, half, r] = out[span]
            stat[t, half] = jnp.where(
                spread == r, top[span], jnp.where(spread == requests + r, total[span], stat[t, half]))

    def compute(t):
        stat[t] = jnp.zeros(stat.shape[1:], jnp.float32)
        if requests % 2 == 0:
            def pair(i, carry):
                one(t, 2 * i)
                one(t, 2 * i + 1)
                return carry
            lax.fori_loop(0, requests // 2, pair, 0)
        else:
            def single(i, carry):
                one(t, i)
                return carry
            lax.fori_loop(0, requests, single, 0)
        for copy in results(t, 1 - k):
            go(copy)

    def merge(t):
        for copy in results(t, k):
            copy.wait_recv()
        mine, other = stat[t, k], core_stat[t]
        new = jnp.zeros((rows, LANES), jnp.float32)
        for r in range(requests):
            top_a, top_b = mine[:, r : r + 1], other[:, r : r + 1]
            sum_a, sum_b = mine[:, requests + r : requests + r + 1], other[:, requests + r : requests + r + 1]
            top = jnp.maximum(top_a, top_b)
            keep_a, keep_b = jnp.exp(top_a - top), jnp.exp(top_b - top)
            block = keep_a * part[t, k, r].astype(jnp.float32) + keep_b * core_part[t, r].astype(jnp.float32)
            block = block.astype(merged.dtype)
            if t == 0:
                got_ref[0, r] = block
            else:
                merged[t, r] = block
            new = jnp.where(
                spread == r, top, jnp.where(spread == requests + r, keep_a * sum_a + keep_b * sum_b, new))
        if t == 0:
            got_stat_ref[0] = new
        else:
            merged_stat[t] = new
            for copy in returns(t):
                go(copy)

    forward(0)
    heads[0, k] = q_ref[...]
    for t in range(depth):
        if t > 0:
            q_line(t).wait_recv()
            forward(t)
            merge(t - 1)
        q_core(t, 1 - k).wait_recv()
        compute(t)
    merge(depth - 1)
    for t in range(1, depth):
        for copy in returns(t):
            copy.wait_recv()
    for copy in sent:
        copy.wait_send()


def attend(q, cache, live, depth, scale, collective_id):
    requests, rows, features = q.shape
    sems = pltpu.SemaphoreType.DMA
    blocks = (depth, requests, rows, LATENT_WIDTH)
    stats = (depth, rows, LANES)
    vmem = pl.BlockSpec(memory_space=pltpu.VMEM)
    return pl.pallas_call(
        functools.partial(attend_kernel, depth, scale),
        out_shape=(jax.ShapeDtypeStruct(blocks, jnp.bfloat16), jax.ShapeDtypeStruct(stats, jnp.float32)),
        in_specs=[vmem] * 3,
        out_specs=(vmem, vmem),
        scratch_shapes=[
            pltpu.VMEM((depth, 2, requests, rows, features), jnp.bfloat16),
            pltpu.VMEM((depth, 2, requests, rows, LATENT_WIDTH), jnp.bfloat16),
            pltpu.VMEM((depth, 2, rows, LANES), jnp.float32),
            pltpu.VMEM(blocks, jnp.bfloat16),
            pltpu.VMEM(stats, jnp.float32),
            pltpu.VMEM(blocks, jnp.bfloat16),
            pltpu.VMEM(stats, jnp.float32),
        ] + [sems((depth,))] * 4 + [sems((depth, 2))] * 4,
        compiler_params=pltpu.CompilerParams(
            collective_id=collective_id, has_side_effects=True, vmem_limit_bytes=48 * 2**20),
    )(q, cache, live)


def local(
    query,
    cache,
    new_keys,
    lengths,
    value_up_weight,
    w_out,
    residual,
    norm_gain,
    w_router,
    routes,
    w_gate,
    w_up,
    w_down,
):
    score_scale = (QK_NOPE + ROTARY_WIDTH) ** (-0.5)
    ctx_count = lax.axis_size("ctx")
    group_count = lax.axis_size("group")
    depth = ctx_count // 2
    ctx_index = lax.axis_index("ctx")
    group_index = lax.axis_index("group")
    grouped_rows, local_heads, features = query.shape
    request_batch = lengths.shape[0]
    draft_tokens = grouped_rows // request_batch
    block_len = cache.shape[1]
    positions = ctx_index * block_len + jnp.arange(block_len, dtype=jnp.int32)
    live = (positions[None, :] < lengths[:, None]).astype(jnp.float32)[:, None, :]
    folded = query.reshape(request_batch, draft_tokens * local_heads, features)
    results, stats = attend(folded, cache, live, depth, score_scale, 3)
    stats = stats.transpose(0, 2, 1)
    arrived = (
        stats[:, :request_batch].reshape(depth, grouped_rows, local_heads),
        stats[:, request_batch : 2 * request_batch].reshape(depth, grouped_rows, local_heads),
        results.reshape(depth, grouped_rows, local_heads, LATENT_WIDTH),
    )
    cache_max = jnp.max(arrived[0], axis=0)
    factors = jnp.exp(arrived[0] - cache_max[None])
    cache_sum = jnp.sum(factors * arrived[1], axis=0)
    cache_result = jnp.sum(factors[..., None] * arrived[2].astype(jnp.float32), axis=0)
    own_query = query.reshape(request_batch, draft_tokens, local_heads, features)
    recent_keys = new_keys.reshape(request_batch, draft_tokens, features)
    near_scores = score_scale * jnp.einsum(
        "rqhd,rjd->rqhj", own_query, recent_keys, preferred_element_type=jnp.float32
    )
    causal = (
        jnp.arange(draft_tokens, dtype=jnp.int32)[None, :]
        <= jnp.arange(draft_tokens, dtype=jnp.int32)[:, None]
    )
    causal = causal[None, :, None, :]
    near_max = jnp.max(jnp.where(causal, near_scores, neg_floor), axis=-1)
    shaped_max = cache_max.reshape(request_batch, draft_tokens, local_heads)
    joint_max = jnp.maximum(shaped_max, near_max)
    cache_rescale = jnp.exp(shaped_max - joint_max)
    nearby_probability = jnp.exp(jnp.where(causal, near_scores - joint_max[..., None], neg_floor))
    denominator = cache_sum.reshape(
        request_batch, draft_tokens, local_heads
    ) * cache_rescale + jnp.sum(nearby_probability, axis=-1)
    softmax_numerator = cache_result.reshape(
        request_batch, draft_tokens, local_heads, LATENT_WIDTH
    ) * cache_rescale[..., None] + jnp.einsum(
        "rqhj,rjk->rqhk",
        nearby_probability,
        recent_keys[:, :, :LATENT_WIDTH].astype(jnp.float32),
        precision=lax.Precision.HIGHEST,
    )
    latent_vector = (
        (softmax_numerator / denominator[..., None])
        .astype(jnp.bfloat16)
        .reshape(grouped_rows, local_heads, LATENT_WIDTH)
    )
    per_head_values = jnp.einsum(
        "gxj,xjs->gxs", latent_vector, value_up_weight, preferred_element_type=jnp.float32
    )
    per_head_values = per_head_values.astype(jnp.bfloat16).reshape(
        grouped_rows, local_heads * VALUE_HEAD_WIDTH
    )
    row_count, model_width = residual.shape
    block = row_count * model_width // LANES
    share = jnp.dot(per_head_values, w_out, preferred_element_type=jnp.float32).astype(jnp.bfloat16)
    share = share.reshape(1, depth, 2, block, LANES).transpose(2, 0, 1, 3, 4)
    attention = summed_rows(share, 0).reshape(row_count, model_width)
    attn_out = attention.astype(jnp.bfloat16)
    stream = (residual.astype(jnp.float32) + attention).astype(jnp.bfloat16)
    stream_wide = stream.astype(jnp.float32)
    mean_square = jnp.mean(stream_wide * stream_wide, axis=-1, keepdims=True)
    normed = (stream_wide * lax.rsqrt(mean_square + norm_eps) * norm_gain).astype(jnp.bfloat16)
    expert_ids = jnp.arange(EXPERTS, dtype=jnp.int32)
    chosen = jnp.sum((routes[:, :, None] == expert_ids).astype(jnp.bfloat16), axis=1).reshape(1, -1)
    chosen = jnp.pad(chosen, ((0, 15), (0, LANES - row_count * EXPERTS)))
    sent = jnp.concatenate([normed.reshape(block, LANES), chosen], axis=0)
    gathered = all_rows(sent, group_count, depth, 1).transpose(1, 2, 0, 3, 4)
    device_count = group_count * ctx_count
    rows = gathered[..., :block, :].reshape(device_count * row_count, model_width)
    gate_values = jax.nn.sigmoid(jnp.dot(rows, w_router, preferred_element_type=jnp.float32))
    chosen = gathered[..., block, : row_count * EXPERTS].reshape(device_count * row_count, EXPERTS)
    chosen = chosen.astype(jnp.float32)
    picked = chosen * gate_values
    expert = (group_index * ctx_count + ctx_index) // (device_count // EXPERTS)
    own = (expert_ids == expert).astype(jnp.float32)
    coefficient = (
        route_scale * jnp.sum(picked * own, axis=-1, keepdims=True) / jnp.sum(picked, axis=-1, keepdims=True)
    )
    gate_sum = jnp.dot(rows, w_gate, preferred_element_type=jnp.float32)
    up_sum = jnp.dot(rows, w_up, preferred_element_type=jnp.float32)
    hidden = (jax.nn.silu(gate_sum) * up_sum).astype(jnp.bfloat16)
    mixed = coefficient * jnp.dot(hidden, w_down, preferred_element_type=jnp.float32)
    mixed = mixed.astype(jnp.bfloat16).reshape(group_count, depth, 2, block, LANES)
    expert_mix = summed_rows(mixed.transpose(2, 0, 1, 3, 4), 2).reshape(row_count, model_width)
    layer_out = (stream_wide + expert_mix).astype(jnp.bfloat16)
    return (attn_out, layer_out)


def solution(mesh):
    return jax.shard_map(
        local,
        mesh=mesh,
        in_specs=(
            P("group", "ctx", None),
            P("group", "ctx", None),
            P("group", None),
            P("group"),
            P("ctx", None, None),
            P("ctx", None),
            P(("group", "ctx"), None),
            P(),
            P(),
            P(("group", "ctx"), None),
            P(None, ("group", "ctx")),
            P(None, ("group", "ctx")),
            P(("group", "ctx"), None),
        ),
        out_specs=(P(("group", "ctx"), None), P(("group", "ctx"), None)),
        check_vma=False,
    )
```

```python
import functools

import jax
import jax.numpy as jnp
from jax import lax
from jax.experimental import pallas as pl
from jax.experimental.pallas import tpu as pltpu
from jax.sharding import PartitionSpec as P

LATENT_WIDTH = 512
ROTARY_WIDTH = 64
QK_NOPE = 128
VALUE_HEAD_WIDTH = 128
EXPERTS = 16
LANES = 128
MESH = pl.DeviceIdType.MESH


neg_floor = -1e30
route_scale = 2.5
norm_eps = 1e-06


def enter(peers):
    barrier = pltpu.get_barrier_semaphore()
    for peer in peers:
        pl.semaphore_signal(barrier, inc=1, device_id=peer, device_id_type=MESH)
    pl.semaphore_wait(barrier, len(peers))


def place(planes, depth):
    g = lax.axis_index("group")
    c = lax.axis_index("ctx")
    z, k = c // 2, c % 2
    partner = (g, z * 2 + 1 - k)
    plane = [(lax.rem(g + d, lax.axis_size("group")), c) for d in range(1, planes)]
    line = [(g, lax.rem(z + d, depth) * 2 + k) for d in range(1, depth)]
    return g, z, k, partner, plane, line


def gather_kernel(planes, depth, x_ref, out_ref, core_send, core_recv, plane_send, plane_recv, line_send, line_recv):
    g, z, k, partner, plane, line = place(planes, depth)
    enter([partner] + plane + line)
    out_ref[k, g, z] = x_ref[...]

    def line_copy(d, slot):
        return pltpu.make_async_remote_copy(
            src_ref=x_ref, dst_ref=slot, send_sem=line_send.at[d], recv_sem=line_recv.at[d],
            device_id=line[d - 1], device_id_type=MESH)

    def plane_copy(p, d, src, slot):
        return pltpu.make_async_remote_copy(
            src_ref=src, dst_ref=slot, send_sem=plane_send.at[p, d], recv_sem=plane_recv.at[p, d],
            device_id=plane[p - 1], device_id_type=MESH)

    def core_copy(p, d, src, slot):
        return pltpu.make_async_remote_copy(
            src_ref=src, dst_ref=slot, send_sem=core_send.at[p, d], recv_sem=core_recv.at[p, d],
            device_id=partner, device_id_type=MESH)

    sent = []
    for d in range(1, depth):
        copy = line_copy(d, out_ref.at[k, g, z])
        copy.start()
        sent.append(copy)
    for d in range(depth):
        zd = lax.rem(z - d + depth, depth)
        slot = out_ref.at[k, g, zd]
        src = x_ref if d == 0 else slot
        if d > 0:
            line_copy(d, slot).wait_recv()
        for p in range(1, planes):
            copy = plane_copy(p, d, src, slot)
            copy.start()
            sent.append(copy)
        copy = core_copy(0, d, src, slot)
        copy.start()
        sent.append(copy)
    for d in range(depth):
        zd = lax.rem(z - d + depth, depth)
        for p in range(1, planes):
            slot = out_ref.at[k, lax.rem(g - p + planes, planes), zd]
            plane_copy(p, d, slot, slot).wait_recv()
            copy = core_copy(p, d, slot, slot)
            copy.start()
            sent.append(copy)
    for d in range(depth):
        zd = lax.rem(z - d + depth, depth)
        for p in range(planes):
            slot = out_ref.at[1 - k, lax.rem(g - p + planes, planes), zd]
            core_copy(p, d, slot, slot).wait_recv()
    for copy in sent:
        copy.wait_send()


def all_rows(x, planes, depth, collective_id):
    sems = pltpu.SemaphoreType.DMA
    return pl.pallas_call(
        functools.partial(gather_kernel, planes, depth),
        out_shape=jax.ShapeDtypeStruct((2, planes, depth) + x.shape, x.dtype),
        in_specs=[pl.BlockSpec(memory_space=pltpu.VMEM)],
        out_specs=pl.BlockSpec(memory_space=pltpu.VMEM),
        scratch_shapes=[sems((planes, depth))] * 4 + [sems((depth,))] * 2,
        compiler_params=pltpu.CompilerParams(
            collective_id=collective_id, has_side_effects=True, vmem_limit_bytes=32 * 2**20),
    )(x)


def scatter_kernel(planes, depth, x_ref, out_ref, core_buf, plane_out, plane_buf, line_out, line_buf,
                   core_send, core_recv, plane_send, plane_recv, line_send, line_recv):
    g, z, k, partner, plane, line = place(planes, depth)
    enter([partner] + plane + line)
    at = g if planes > 1 else 0
    wide = lambda block: block.astype(jnp.float32)

    sent = []
    order = list(range(1, planes)) + [0]
    core = {}
    for p in order:
        gp = lax.rem(at + p, planes)
        copy = pltpu.make_async_remote_copy(
            src_ref=x_ref.at[1 - k, gp], dst_ref=core_buf.at[p], send_sem=core_send.at[p], recv_sem=core_recv.at[p],
            device_id=partner, device_id_type=MESH)
        copy.start()
        core[p] = copy
        sent.append(copy)
    planes_in = {}
    for p in order[:-1]:
        gp = lax.rem(at + p, planes)
        core[p].wait_recv()
        for d in range(depth):
            plane_out[p, d] = (wide(x_ref[k, gp, d]) + wide(core_buf[p, d])).astype(plane_out.dtype)
        copy = pltpu.make_async_remote_copy(
            src_ref=plane_out.at[p], dst_ref=plane_buf.at[p], send_sem=plane_send.at[p], recv_sem=plane_recv.at[p],
            device_id=plane[p - 1], device_id_type=MESH)
        copy.start()
        planes_in[p] = copy
        sent.append(copy)
    core[0].wait_recv()
    for p in order[:-1]:
        planes_in[p].wait_recv()

    def total(zd):
        block = wide(x_ref[k, at, zd]) + wide(core_buf[0, zd])
        for p in range(1, planes):
            block = block + wide(plane_buf[p, zd])
        return block

    lines_in = []
    for d in range(1, depth):
        line_out[d] = total(lax.rem(z + d, depth)).astype(line_out.dtype)
        copy = pltpu.make_async_remote_copy(
            src_ref=line_out.at[d], dst_ref=line_buf.at[d], send_sem=line_send.at[d], recv_sem=line_recv.at[d],
            device_id=line[d - 1], device_id_type=MESH)
        copy.start()
        lines_in.append(copy)
        sent.append(copy)
    result = total(z)
    for d in range(1, depth):
        lines_in[d - 1].wait_recv()
        result = result + wide(line_buf[d])
    out_ref[...] = result
    for copy in sent:
        copy.wait_send()


def summed_rows(x, collective_id):
    _, planes, depth, *block = x.shape
    block = tuple(block)
    sems = pltpu.SemaphoreType.DMA
    return pl.pallas_call(
        functools.partial(scatter_kernel, planes, depth),
        out_shape=jax.ShapeDtypeStruct(block, jnp.float32),
        in_specs=[pl.BlockSpec(memory_space=pltpu.VMEM)],
        out_specs=pl.BlockSpec(memory_space=pltpu.VMEM),
        scratch_shapes=[
            pltpu.VMEM((planes, depth) + block, x.dtype),
            pltpu.VMEM((planes, depth) + block, x.dtype),
            pltpu.VMEM((planes, depth) + block, x.dtype),
            pltpu.VMEM((depth,) + block, x.dtype),
            pltpu.VMEM((depth,) + block, x.dtype),
        ] + [sems((planes,))] * 4 + [sems((depth,))] * 2,
        compiler_params=pltpu.CompilerParams(
            collective_id=collective_id, has_side_effects=True, vmem_limit_bytes=32 * 2**20),
    )(x)


def attend_kernel(depth, scale, q_ref, cache_ref, live_ref, got_ref, got_stat_ref, heads, held_cache, part, stat, core_part,
                  core_stat, merged, merged_stat, cache_sem, q_line_send, q_line_recv, q_core_send, q_core_recv, core_send, core_recv,
                  line_send, line_recv):
    g = lax.axis_index("group")
    c = lax.axis_index("ctx")
    z, k = c // 2, c % 2
    requests, rows, _ = q_ref.shape
    middle = requests // 2
    chunks = (range(middle), range(middle, requests))
    spread = lax.broadcasted_iota(jnp.int32, (rows, LANES), 1)

    def chip(t):
        at, bit = z, 1
        while bit <= t:
            if t & bit:
                at = at + bit - 2 * bit * ((z // bit) % 2)
            bit *= 2
        return at

    partner = (g, z * 2 + 1 - k)
    owners = [(g, chip(t) * 2 + k) for t in range(depth)]
    enter([partner] + owners[1:])

    def remote(src, dst, send, recv, device):
        return pltpu.make_async_remote_copy(
            src_ref=src, dst_ref=dst, send_sem=send, recv_sem=recv, device_id=device, device_id_type=MESH)

    sent = []

    def go(copy):
        copy.start()
        sent.append(copy)

    def held(t):
        return q_ref if t == 0 else heads.at[t, k]

    def q_line(t):
        bit = 1 << (t.bit_length() - 1)
        return remote(held(t - bit), heads.at[t, k], q_line_send.at[t], q_line_recv.at[t], owners[bit])

    def q_core(t, half):
        return remote(held(t), heads.at[t, half], q_core_send.at[t], q_core_recv.at[t], partner)

    def results(t, h, half):
        span = pl.ds(chunks[h][0], len(chunks[h]))
        return (
            remote(part.at[t, half, span], core_part.at[t, span], core_send.at[t, h, 0], core_recv.at[t, h, 0], partner),
            remote(stat.at[t, h, half], core_stat.at[t, h], core_send.at[t, h, 1], core_recv.at[t, h, 1], partner),
        )

    def returns(t, h):
        span = pl.ds(chunks[h][0], len(chunks[h]))
        block = remote(
            merged.at[t, span], got_ref.at[t, span], line_send.at[t, h], line_recv.at[t, h], owners[t])
        if h == 0:
            return (block,)
        return (block, remote(merged_stat.at[t], got_stat_ref.at[t], line_send.at[t, 2], line_recv.at[t, 2], owners[t]))

    def relay(t, bit):
        while t + bit < depth:
            go(q_line(t + bit))
            bit *= 2

    def one(t, r):
        both = jnp.concatenate([heads[t, 0, r], heads[t, 1, r]], axis=0)
        keys = held_cache[r]
        score = scale * jnp.dot(both, keys, preferred_element_type=jnp.float32)
        live = live_ref[r] > 0.0
        top = jnp.max(jnp.where(live, score, neg_floor), axis=-1, keepdims=True)
        prob = jnp.exp(jnp.where(live, score - top, neg_floor))
        total = jnp.sum(prob, axis=-1, keepdims=True)
        out = lax.dot_general(
            prob.astype(jnp.bfloat16), keys[:LATENT_WIDTH], (((1,), (1,)), ((), ())),
            preferred_element_type=jnp.float32)
        out = out.astype(part.dtype)
        for half in range(2):
            part[t, half, r] = out[half * rows : (half + 1) * rows]
        return top, total

    def compute(t, h, between):
        stats = jnp.zeros((2 * rows, LANES), jnp.float32)
        lanes = lax.broadcasted_iota(jnp.int32, (2 * rows, LANES), 1)
        for i, r in enumerate(chunks[h]):
            if i == len(chunks[h]) // 2:
                between()
            top, total = one(t, r)
            stats = jnp.where(lanes == r, top, jnp.where(lanes == requests + r, total, stats))
        for half in range(2):
            stat[t, h, half] = stats[half * rows : (half + 1) * rows]
        for copy in results(t, h, 1 - k):
            go(copy)

    def merge(t, h):
        for copy in results(t, h, k):
            copy.wait_recv()
        mine, other = stat[t, h, k], core_stat[t, h]
        stat_ref = got_stat_ref if t == 0 else merged_stat
        new = jnp.zeros((rows, LANES), jnp.float32) if h == 0 else stat_ref[t]
        for r in chunks[h]:
            top_a, top_b = mine[:, r : r + 1], other[:, r : r + 1]
            sum_a, sum_b = mine[:, requests + r : requests + r + 1], other[:, requests + r : requests + r + 1]
            top = jnp.maximum(top_a, top_b)
            keep_a, keep_b = jnp.exp(top_a - top), jnp.exp(top_b - top)
            block = keep_a * part[t, k, r].astype(jnp.float32) + keep_b * core_part[t, r].astype(jnp.float32)
            block = block.astype(merged.dtype)
            if t == 0:
                got_ref[0, r] = block
            else:
                merged[t, r] = block
            new = jnp.where(
                spread == r, top, jnp.where(spread == requests + r, keep_a * sum_a + keep_b * sum_b, new))
        stat_ref[t] = new
        if t > 0:
            for copy in returns(t, h):
                go(copy)

    go(q_core(0, k))
    if depth > 1:
        go(q_line(1))
    load = pltpu.make_async_copy(cache_ref, held_cache, cache_sem)
    load.start()
    heads[0, k] = q_ref[...]
    load.wait()
    for t in range(depth):
        if t > 0:
            q_line(t).wait_recv()
            go(q_core(t, k))
            relay(t, 1 << t.bit_length())
            merge(t - 1, 1)
        q_core(t, 1 - k).wait_recv()
        compute(t, 0, functools.partial(relay, 0, 2) if t == 0 else lambda: None)
        compute(t, 1, functools.partial(merge, t, 0))
    merge(depth - 1, 1)
    for t in range(1, depth):
        for copy in returns(t, 0) + returns(t, 1):
            copy.wait_recv()
    for copy in sent:
        copy.wait_send()


def attend(q, cache, live, depth, scale, collective_id):
    requests, rows, features = q.shape
    sems = pltpu.SemaphoreType.DMA
    blocks = (depth, requests, rows, LATENT_WIDTH)
    stats = (depth, rows, LANES)
    vmem = pl.BlockSpec(memory_space=pltpu.VMEM)
    return pl.pallas_call(
        functools.partial(attend_kernel, depth, scale),
        out_shape=(jax.ShapeDtypeStruct(blocks, jnp.bfloat16), jax.ShapeDtypeStruct(stats, jnp.float32)),
        in_specs=[vmem, pl.BlockSpec(memory_space=pl.ANY), vmem],
        out_specs=(vmem, vmem),
        scratch_shapes=[
            pltpu.VMEM((depth, 2, requests, rows, features), jnp.bfloat16),
            pltpu.VMEM(cache.shape, jnp.bfloat16),
            pltpu.VMEM((depth, 2, requests, rows, LATENT_WIDTH), jnp.bfloat16),
            pltpu.VMEM((depth, 2, 2, rows, LANES), jnp.float32),
            pltpu.VMEM(blocks, jnp.bfloat16),
            pltpu.VMEM((depth, 2, rows, LANES), jnp.float32),
            pltpu.VMEM(blocks, jnp.bfloat16),
            pltpu.VMEM(stats, jnp.float32),
            sems,
        ] + [sems((depth,))] * 4 + [sems((depth, 2, 2))] * 2 + [sems((depth, 3))] * 2,
        compiler_params=pltpu.CompilerParams(
            collective_id=collective_id, has_side_effects=True, vmem_limit_bytes=48 * 2**20),
    )(q, cache, live)


def local(
    query,
    cache,
    new_keys,
    lengths,
    value_up_weight,
    w_out,
    residual,
    norm_gain,
    w_router,
    routes,
    w_gate,
    w_up,
    w_down,
):
    score_scale = (QK_NOPE + ROTARY_WIDTH) ** (-0.5)
    ctx_count = lax.axis_size("ctx")
    group_count = lax.axis_size("group")
    depth = ctx_count // 2
    ctx_index = lax.axis_index("ctx")
    group_index = lax.axis_index("group")
    grouped_rows, local_heads, features = query.shape
    request_batch = lengths.shape[0]
    draft_tokens = grouped_rows // request_batch
    block_len = cache.shape[1]
    positions = ctx_index * block_len + jnp.arange(block_len, dtype=jnp.int32)
    live = (positions[None, :] < lengths[:, None]).astype(jnp.float32)[:, None, :]
    folded = query.reshape(request_batch, draft_tokens * local_heads, features)
    results, stats = attend(folded, cache.transpose(0, 2, 1), live, depth, score_scale, 3)
    stats = stats.transpose(0, 2, 1)
    arrived = (
        stats[:, :request_batch].reshape(depth, grouped_rows, local_heads),
        stats[:, request_batch : 2 * request_batch].reshape(depth, grouped_rows, local_heads),
        results.reshape(depth, grouped_rows, local_heads, LATENT_WIDTH),
    )
    cache_max = jnp.max(arrived[0], axis=0)
    factors = jnp.exp(arrived[0] - cache_max[None])
    cache_sum = jnp.sum(factors * arrived[1], axis=0)
    cache_result = jnp.sum(factors[..., None] * arrived[2].astype(jnp.float32), axis=0)
    own_query = query.reshape(request_batch, draft_tokens, local_heads, features)
    recent_keys = new_keys.reshape(request_batch, draft_tokens, features)
    near_scores = score_scale * jnp.einsum(
        "rqhd,rjd->rqhj", own_query, recent_keys, preferred_element_type=jnp.float32
    )
    causal = (
        jnp.arange(draft_tokens, dtype=jnp.int32)[None, :]
        <= jnp.arange(draft_tokens, dtype=jnp.int32)[:, None]
    )
    causal = causal[None, :, None, :]
    near_max = jnp.max(jnp.where(causal, near_scores, neg_floor), axis=-1)
    shaped_max = cache_max.reshape(request_batch, draft_tokens, local_heads)
    joint_max = jnp.maximum(shaped_max, near_max)
    cache_rescale = jnp.exp(shaped_max - joint_max)
    nearby_probability = jnp.exp(jnp.where(causal, near_scores - joint_max[..., None], neg_floor))
    denominator = cache_sum.reshape(
        request_batch, draft_tokens, local_heads
    ) * cache_rescale + jnp.sum(nearby_probability, axis=-1)
    softmax_numerator = cache_result.reshape(
        request_batch, draft_tokens, local_heads, LATENT_WIDTH
    ) * cache_rescale[..., None] + jnp.einsum(
        "rqhj,rjk->rqhk",
        nearby_probability,
        recent_keys[:, :, :LATENT_WIDTH].astype(jnp.float32),
        precision=lax.Precision.HIGHEST,
    )
    latent_vector = (
        (softmax_numerator / denominator[..., None])
        .astype(jnp.bfloat16)
        .reshape(grouped_rows, local_heads, LATENT_WIDTH)
    )
    per_head_values = jnp.einsum(
        "gxj,xjs->gxs", latent_vector, value_up_weight, preferred_element_type=jnp.float32
    )
    per_head_values = per_head_values.astype(jnp.bfloat16).reshape(
        grouped_rows, local_heads * VALUE_HEAD_WIDTH
    )
    row_count, model_width = residual.shape
    block = row_count * model_width // LANES
    share = jnp.dot(per_head_values, w_out, preferred_element_type=jnp.float32).astype(jnp.bfloat16)
    share = share.reshape(1, depth, 2, block, LANES).transpose(2, 0, 1, 3, 4)
    attention = summed_rows(share, 0).reshape(row_count, model_width)
    attn_out = attention.astype(jnp.bfloat16)
    stream = (residual.astype(jnp.float32) + attention).astype(jnp.bfloat16)
    stream_wide = stream.astype(jnp.float32)
    mean_square = jnp.mean(stream_wide * stream_wide, axis=-1, keepdims=True)
    normed = (stream_wide * lax.rsqrt(mean_square + norm_eps) * norm_gain).astype(jnp.bfloat16)
    expert_ids = jnp.arange(EXPERTS, dtype=jnp.int32)
    chosen = jnp.sum((routes[:, :, None] == expert_ids).astype(jnp.bfloat16), axis=1).reshape(1, -1)
    chosen = jnp.pad(chosen, ((0, 15), (0, LANES - row_count * EXPERTS)))
    sent = jnp.concatenate([normed.reshape(block, LANES), chosen], axis=0)
    gathered = all_rows(sent, group_count, depth, 1).transpose(1, 2, 0, 3, 4)
    device_count = group_count * ctx_count
    rows = gathered[..., :block, :].reshape(device_count * row_count, model_width)
    gate_values = jax.nn.sigmoid(jnp.dot(rows, w_router, preferred_element_type=jnp.float32))
    chosen = gathered[..., block, : row_count * EXPERTS].reshape(device_count * row_count, EXPERTS)
    chosen = chosen.astype(jnp.float32)
    picked = chosen * gate_values
    expert = (group_index * ctx_count + ctx_index) // (device_count // EXPERTS)
    own = (expert_ids == expert).astype(jnp.float32)
    coefficient = (
        route_scale * jnp.sum(picked * own, axis=-1, keepdims=True) / jnp.sum(picked, axis=-1, keepdims=True)
    )
    gate_sum = jnp.dot(rows, w_gate, preferred_element_type=jnp.float32)
    up_sum = jnp.dot(rows, w_up, preferred_element_type=jnp.float32)
    hidden = (jax.nn.silu(gate_sum) * up_sum).astype(jnp.bfloat16)
    mixed = coefficient * jnp.dot(hidden, w_down, preferred_element_type=jnp.float32)
    mixed = mixed.astype(jnp.bfloat16).reshape(group_count, depth, 2, block, LANES)
    expert_mix = summed_rows(mixed.transpose(2, 0, 1, 3, 4), 2).reshape(row_count, model_width)
    layer_out = (stream_wide + expert_mix).astype(jnp.bfloat16)
    return (attn_out, layer_out)


def solution(mesh):
    return jax.shard_map(
        local,
        mesh=mesh,
        in_specs=(
            P("group", "ctx", None),
            P("group", "ctx", None),
            P("group", None),
            P("group"),
            P("ctx", None, None),
            P("ctx", None),
            P(("group", "ctx"), None),
            P(),
            P(),
            P(("group", "ctx"), None),
            P(None, ("group", "ctx")),
            P(None, ("group", "ctx")),
            P(("group", "ctx"), None),
        ),
        out_specs=(P(("group", "ctx"), None), P(("group", "ctx"), None)),
        check_vma=False,
    )
```
